32 devices in a mesh: blk: 2 (over y), wide: 16 (over z, x, core).
Axes of the slice: x: 2, y: 2, z: 4, core: 2. Of those that a mesh axis runs over, the one named last changes fastest.
Arguments:
- series: bfloat16 [5632, 640], P(('blk', 'wide'))
- scrub_mask: int32 [640], replicated, may hold values from 0 to 1, as said below
- seed_index: int32 [256], P(('blk', 'wide')), may hold values from 0 to 5631, as said below
Outputs:
- dispersion: bfloat16 [2, 2816, 256], P(None, 'wide', 'blk')
- statistic: bfloat16 [2, 2816, 256], P(None, 'wide', 'blk')
The draws below stay inside these ranges and needn't reach their ends.
Inputs may be any that keep to these rules, and one draw needn't show every extreme that they name: Entry i of seed_index lies among the rows (i // 8) * 176 to (i // 8 + 1) * 176 - 1, and the 8 entries of one such block are distinct. `scrub_mask`: every frame of even position is kept.
All inputs are finite; a program needn't handle non-finite values.
Results may differ from the reference program's by a relative error of at most 0.0057.
Values may be sent and summed in bfloat16 or wider, within the bound.
A program may use at most 128 MiB of HBM per device.

```python
import math
import jax
import jax.numpy as jnp
from jax import lax

SEED_DEV = 8
TGT_DEV = 176
FRAMES = 640
WIN = 60
STRIDE = 30
NWIN = 20
SEEDS = 256
TARGETS = 5632
N_BLK = 2
N_WIDE = 16


def draw_series(key, part):
    key_scale, key_offset, key_gain, key_noise = jax.random.split(key, 4)
    row_scale = jnp.exp(jax.random.uniform(key_scale, (TARGETS, 1), minval=0.0, maxval=math.log(10.0)))
    offset = jax.random.uniform(key_offset, (TARGETS, 1), minval=-3.0, maxval=3.0)
    frame_gain = jnp.exp(jax.random.uniform(key_gain, (1, FRAMES), minval=-0.7, maxval=0.7))
    fluctuation = jax.random.normal(key_noise, (TARGETS, FRAMES))
    return (offset + row_scale * frame_gain * fluctuation).astype(jnp.bfloat16)


def draw_scrub_mask(key, part):
    coin_flips = jax.random.randint(key, (FRAMES,), 0, 4)
    position = jnp.arange(FRAMES, dtype=jnp.int32)
    return jnp.where((position % 2 == 0) | (coin_flips != 0), 1, 0).astype(jnp.int32)


def pick_block(block_key):
    return jax.random.permutation(block_key, TGT_DEV)[:SEED_DEV]


def draw_seed_index(key, part):
    block_count = SEEDS // SEED_DEV
    block_keys = jax.random.split(key, block_count)
    chosen = jax.vmap(pick_block)(block_keys).astype(jnp.int32)
    offsets = jnp.arange(block_count, dtype=jnp.int32)[:, None] * TGT_DEV
    return (chosen + offsets).reshape(SEEDS).astype(jnp.int32)


def setup_inputs(seed: int = 0) -> dict:
    key_of = jax.random.split(jax.random.key(seed), 4)
    return {
        "series": draw_series(jax.random.fold_in(key_of[3], 71), 0),
        "scrub_mask": draw_scrub_mask(jax.random.fold_in(key_of[3], 71), 0),
        "seed_index": draw_seed_index(jax.random.fold_in(key_of[3], 71), 0),
    }


EPSILON = 1e-05
CLIP_LEVEL = 0.99

def fisher_of(values):
    clipped = jnp.clip(values, -CLIP_LEVEL, CLIP_LEVEL)
    return 0.5 * (jnp.log(1.0 + clipped) - jnp.log(1.0 - clipped))

def prepare(raw_rows, scrub_mask):
    values = raw_rows.astype(jnp.float32)
    row_count = values.shape[0]
    weight = scrub_mask.astype(jnp.float32)
    covered = STRIDE * (NWIN + 1)
    pieces = values[:, :covered].reshape(row_count, NWIN + 1, STRIDE)
    framed = jnp.concatenate([pieces[:, :-1], pieces[:, 1:]], axis=2)
    mask_pieces = weight[:covered].reshape(NWIN + 1, STRIDE)
    mask_framed = jnp.concatenate([mask_pieces[:-1], mask_pieces[1:]], axis=1)
    valid_count = lax.optimization_barrier(jnp.sum(mask_framed, axis=1))
    centre = lax.optimization_barrier(jnp.sum(framed * mask_framed, axis=2)) / valid_count
    centred = (framed - centre[:, :, None]) * mask_framed
    spread = lax.optimization_barrier(jnp.sum(centred * centred, axis=2))
    windows = (centred * lax.rsqrt(spread + EPSILON)[:, :, None]).astype(jnp.bfloat16)
    total_valid = jnp.sum(weight)
    mean_all = lax.optimization_barrier(jnp.sum(values * weight, axis=1)) / total_valid
    centred_all = (values - mean_all[:, None]) * weight
    spread_all = lax.optimization_barrier(jnp.sum(centred_all * centred_all, axis=1))
    whole_std = (centred_all * lax.rsqrt(spread_all + EPSILON)[:, None]).astype(jnp.bfloat16)
    return (windows, whole_std)

def compare_exact(target_windows, target_whole, seed_window, seed_whole, total_valid):
    window_corr = jnp.einsum('tnw,snw->nts', target_windows.astype(jnp.float32), seed_window.astype(jnp.float32), precision=lax.Precision.HIGHEST)
    fisher = fisher_of(window_corr)
    first_moment = lax.optimization_barrier(jnp.mean(fisher, axis=0))
    second = lax.optimization_barrier(jnp.mean(fisher * fisher, axis=0))
    dispersion = ((WIN - 3) * (second - first_moment * first_moment)).astype(jnp.bfloat16)
    static = jnp.einsum('tf,sf->ts', target_whole.astype(jnp.float32), seed_whole.astype(jnp.float32), precision=lax.Precision.HIGHEST)
    statistic = (jnp.sqrt(total_valid - 3.0) * fisher_of(static)).astype(jnp.bfloat16)
    return (dispersion, statistic)

def reference(series, scrub_mask, seed_index):
    target_windows, target_whole = prepare(series, scrub_mask)
    seed_window, seed_whole = prepare(jnp.take(series, seed_index, axis=0), scrub_mask)
    total_valid = jnp.sum(scrub_mask.astype(jnp.float32))
    block_count = TARGETS // TGT_DEV
    grouped_windows = target_windows.reshape(block_count, TGT_DEV, NWIN, WIN)
    grouped_whole = target_whole.reshape(block_count, TGT_DEV, FRAMES)

    def compare_block(block_pair):
        return compare_exact(block_pair[0], block_pair[1], seed_window, seed_whole, total_valid)
    dispersion, statistic = lax.map(compare_block, (grouped_windows, grouped_whole))
    out_shape = (N_BLK, N_WIDE * TGT_DEV, SEEDS)
    return (dispersion.reshape(out_shape), statistic.reshape(out_shape))
```

```python
import functools

import jax
import jax.numpy as jnp
from jax import lax
from jax.experimental import pallas as pl
from jax.experimental.pallas import tpu as pltpu
from jax.sharding import PartitionSpec as P

WIN = 60
STRIDE = 30
NWIN = 20
EPSILON = 1e-05
CLIP_LEVEL = 0.99
LANES = 128
HALF = 64
MESH = pl.DeviceIdType.MESH
NT = (((1,), (1,)), ((), ()))


def iota(shape, dim):
    return lax.broadcasted_iota(jnp.int32, shape, dim)


def piece_of(frame):
    return (frame * 2185) >> 16


def mm(a, b):
    return jnp.dot(a, b, preferred_element_type=jnp.float32)


def log_ratio(values):
    clipped = jnp.clip(values, -CLIP_LEVEL, CLIP_LEVEL)
    return jnp.log(1.0 + clipped) - jnp.log(1.0 - clipped)


def kernel(
    n_blk, n_wide, series, mask, seed_index, dispersion, statistic,
    seed_block, panel, others, pairs, spans, seeds, seed_shift, rhs, lhs, acc1, acc2,
    seed_send, seed_recv, row_send, row_recv,
):
    rows, frames = series.shape
    own = seed_index.shape[0]
    size = n_wide * own
    low = panel.shape[2]
    high = frames - low
    me_b = lax.axis_index("blk")
    me_w = lax.axis_index("wide")

    barrier = pltpu.get_barrier_semaphore()
    for d in range(1, n_wide):
        pl.semaphore_signal(
            barrier, inc=1, device_id=(me_b, lax.rem(me_w + d, n_wide)), device_id_type=MESH
        )
    for d in range(1, n_blk):
        pl.semaphore_signal(
            barrier, inc=1, device_id=(lax.rem(me_b + d, n_blk), me_w), device_id_type=MESH
        )

    base = (me_b * n_wide + me_w) * rows
    row = iota((2 * own, rows), 0) & (own - 1)
    wanted = jnp.zeros((2 * own, rows), jnp.int32)
    for i in range(own):
        wanted = jnp.where(row == i, seed_index[i] - base, wanted)
    pick = jnp.where(iota((2 * own, rows), 1) == wanted, 1.0, 0.0).astype(jnp.bfloat16)
    picked = mm(pick, series[...])
    tail = jnp.concatenate([picked[:, low:], picked[:, : low - high]], axis=1)
    block = jnp.where(iota((2 * own, low), 0) < own, picked[:, :low], tail)
    seed_block[...] = block.astype(jnp.bfloat16)

    pl.semaphore_wait(barrier, n_wide + n_blk - 2)
    seed_copies = []
    for d in range(1, n_wide):
        copy = pltpu.make_async_remote_copy(
            src_ref=seed_block, dst_ref=panel.at[d - 1],
            send_sem=seed_send.at[d - 1], recv_sem=seed_recv.at[d - 1],
            device_id=(me_b, lax.rem(me_w + d, n_wide)), device_id_type=MESH,
        )
        copy.start()
        seed_copies.append(copy)
    row_copies = []
    for d in range(1, n_blk):
        copy = pltpu.make_async_remote_copy(
            src_ref=series, dst_ref=others.at[d - 1],
            send_sem=row_send.at[d - 1], recv_sem=row_recv.at[d - 1],
            device_id=(lax.rem(me_b + d, n_blk), me_w), device_id_type=MESH,
        )
        copy.start()
        row_copies.append(copy)

    weight = mask[...].reshape(1, frames).astype(jnp.float32)
    frame_piece = piece_of(iota((frames, 2 * LANES), 0))
    lane = iota((frames, 2 * LANES), 1)
    wanted_piece = (lane & 31) + (lane >> 7)
    pairs[...] = jnp.where(frame_piece == wanted_piece, 1.0, 0.0).astype(jnp.bfloat16)
    row_piece = piece_of(iota((frames, frames), 0))
    column_piece = piece_of(iota((frames, frames), 1))
    spans[...] = jnp.where(row_piece == column_piece, 1.0, 0.0).astype(jnp.bfloat16)
    weight_rows = jnp.broadcast_to(weight, (16, frames)).astype(jnp.bfloat16)
    counts = mm(weight_rows, pairs[...])
    count1, count2 = counts[:1, :LANES], counts[:1, LANES:]
    count = jnp.maximum(count1 + count2, 1.0)
    between = count1 * count2 / count
    count1, count2 = jnp.maximum(count1, 1.0), jnp.maximum(count2, 1.0)
    inverse_count = 1.0 / jnp.maximum(mm(weight_rows, spans[...])[:1], 1.0)
    total_valid = jnp.sum(weight, axis=1, keepdims=True)

    def stats(values):
        kept = values * weight
        kept16 = kept.astype(jnp.bfloat16)
        sums = mm(kept16, pairs[...])
        sum1, sum2 = sums[:, :LANES], sums[:, LANES:]
        inner = (values - mm(kept16, spans[...]) * inverse_count) * weight
        inner = (inner * inner).astype(jnp.bfloat16)
        inner = mm(inner, pairs[:, :LANES] + pairs[:, LANES:])
        step = sum1 / count1 - sum2 / count2
        spread = inner + between * step * step
        mean = (sum1 + sum2) / count
        mean_all = jnp.sum(kept, axis=1, keepdims=True) / total_valid
        centred = (values - mean_all) * weight
        spread_all = jnp.sum(centred * centred, axis=1, keepdims=True)
        whole = (centred * lax.rsqrt(spread_all + EPSILON)).astype(jnp.bfloat16)
        return mean, lax.rsqrt(spread + EPSILON), whole

    stat_lane = iota((rows, LANES), 1)

    def load_target(block16):
        values = block16.astype(jnp.float32)
        mean, inverse, whole = stats(values)
        inverse_high = inverse.astype(jnp.bfloat16).astype(jnp.float32)
        stat = jnp.where(
            stat_lane < 32, mean, jnp.where(stat_lane < 64, inverse_high, inverse - inverse_high)
        )
        lhs[0, :, :frames] = block16
        shift = pltpu.roll(values, frames - HALF, 1)
        lhs[1, :, :frames] = shift.astype(jnp.bfloat16)
        lhs[0, :, frames:] = stat.astype(jnp.bfloat16)
        return whole

    select_lane = iota((size, LANES), 1)
    for n in range(NWIN):
        rhs[n, size:, :LANES] = jnp.zeros((size, LANES), jnp.bfloat16)
        chosen = (select_lane == 32 + n) | (select_lane == 64 + n)
        rhs[n, size:, LANES:] = jnp.where(chosen, 1.0, 0.0).astype(jnp.bfloat16)

    own_whole = load_target(series[...])

    def unpack(block16, source):
        values = block16.astype(jnp.float32)
        at = pl.ds(pl.multiple_of(source * own, own), own)
        seeds[at, :low] = values[:own]
        seeds[at, low:] = values[own:, :high]

    unpack(seed_block[...], me_w)
    for d in range(1, n_wide):
        seed_copies[d - 1].wait_recv()
        unpack(panel[d - 1], lax.rem(me_w + n_wide - d, n_wide))

    seed_values = seeds[...]
    seed_mean, seed_inverse, seed_whole = stats(seed_values)
    seed_shift[...] = pltpu.roll(seed_values, frames - HALF, 1)
    weight_shift = pltpu.roll(jnp.broadcast_to(weight, (8, frames)), frames - HALF, 1)[:1]
    tile_lane = iota((1, LANES), 1)
    for n in range(NWIN):
        k = n * STRIDE // HALF
        at = slice(k // 2 * LANES, k // 2 * LANES + LANES)
        first = n * STRIDE - k * HALF
        inside = (tile_lane >= first) & (tile_lane < first + WIN)
        kept = jnp.where(inside, (weight_shift if k % 2 else weight)[:, at], 0.0)
        tile = (seed_shift if k % 2 else seeds)[:, at]
        window = (tile - seed_mean[:, n : n + 1]) * kept * seed_inverse[:, n : n + 1]
        window = window.astype(jnp.bfloat16)
        left = jnp.sum(window.astype(jnp.float32), axis=1, keepdims=True)
        rhs[n, :size, :LANES] = window
        rhs[n, :size, LANES:] = jnp.where(select_lane == n, -left, 0.0).astype(jnp.bfloat16)

    scale = jnp.sqrt(total_valid - 3.0) * 0.5

    def compare(whole, slot):
        static = lax.dot_general(whole, seed_whole, NT, preferred_element_type=jnp.float32)
        statistic[slot] = (scale * log_ratio(static)).astype(jnp.bfloat16)
        acc1[...] = jnp.zeros_like(acc1)
        acc2[...] = jnp.zeros_like(acc2)
        group = 4

        def step(i, carry):
            first = second = None
            for g in range(group):
                n = i * group + g
                k = n * STRIDE // HALF
                at = pl.ds(pl.multiple_of(k // 2 * LANES, LANES), LANES)
                left = jnp.concatenate([lhs[k % 2, :, at], lhs[0, :, frames:]], axis=1)
                both = lax.dot_general(left, rhs[n], NT, preferred_element_type=jnp.float32)
                z = log_ratio(both[:, :size] * both[:, size:])
                first = z if g == 0 else first + z
                second = z * z if g == 0 else second + z * z
            acc1[...] += first
            acc2[...] += second
            return carry

        lax.fori_loop(0, NWIN // group, step, 0)
        moment = acc1[...] * (0.5 / NWIN)
        spread = acc2[...] * (0.25 / NWIN) - moment * moment
        dispersion[slot] = ((WIN - 3) * spread).astype(jnp.bfloat16)

    compare(own_whole, me_b)
    for d in range(1, n_blk):
        row_copies[d - 1].wait_recv()
        whole = load_target(others[d - 1])
        compare(whole, lax.rem(me_b + n_blk - d, n_blk))

    for copy in seed_copies + row_copies:
        copy.wait_send()


def solution(mesh):
    n_blk, n_wide = mesh.shape["blk"], mesh.shape["wide"]

    def body(series, scrub_mask, seed_index):
        rows, frames = series.shape
        own = seed_index.shape[0]
        size = n_wide * own
        low = (frames // LANES + 1) // 2 * LANES
        out = jax.ShapeDtypeStruct((n_blk, rows, size), jnp.bfloat16)
        vmem = pl.BlockSpec(memory_space=pltpu.VMEM)
        return pl.pallas_call(
            functools.partial(kernel, n_blk, n_wide),
            out_shape=(out, out),
            in_specs=[vmem, vmem, pl.BlockSpec(memory_space=pltpu.SMEM)],
            out_specs=(vmem, vmem),
            scratch_shapes=[
                pltpu.VMEM((2 * own, low), jnp.bfloat16),
                pltpu.VMEM((n_wide - 1, 2 * own, low), jnp.bfloat16),
                pltpu.VMEM((n_blk - 1, rows, frames), jnp.bfloat16),
                pltpu.VMEM((frames, 2 * LANES), jnp.bfloat16),
                pltpu.VMEM((frames, frames), jnp.bfloat16),
                pltpu.VMEM((size, frames), jnp.float32),
                pltpu.VMEM((size, frames), jnp.float32),
                pltpu.VMEM((NWIN, 2 * size, 2 * LANES), jnp.bfloat16),
                pltpu.VMEM((2, rows, frames + LANES), jnp.bfloat16),
                pltpu.VMEM((rows, size), jnp.float32),
                pltpu.VMEM((rows, size), jnp.float32),
                pltpu.SemaphoreType.DMA((n_wide - 1,)),
                pltpu.SemaphoreType.DMA((n_wide - 1,)),
                pltpu.SemaphoreType.DMA((n_blk - 1,)),
                pltpu.SemaphoreType.DMA((n_blk - 1,)),
            ],
            compiler_params=pltpu.CompilerParams(
                collective_id=0, has_side_effects=True, vmem_limit_bytes=48 * 2**20
            ),
            cost_estimate=pl.CostEstimate(
                flops=n_blk * rows * size * 2 * 1800, bytes_accessed=2**20, transcendentals=0
            ),
        )(series, scrub_mask, seed_index)

    in_specs = (P(("blk", "wide"), None), P(), P(("blk", "wide")))
    out_specs = (P(None, "wide", "blk"), P(None, "wide", "blk"))
    return jax.shard_map(body, mesh=mesh, in_specs=in_specs, out_specs=out_specs, check_vma=False)
```

```python
import functools

import jax
import jax.numpy as jnp
from jax import lax
from jax.experimental import pallas as pl
from jax.experimental.pallas import tpu as pltpu
from jax.sharding import PartitionSpec as P

WIN = 60
STRIDE = 30
NWIN = 20
SPAN = 21
EPSILON = 1e-05
CLIP_LEVEL = 0.99
LANES = 128
HALF = 64
MESH = pl.DeviceIdType.MESH
NT = (((1,), (1,)), ((), ()))


def iota(shape, dim):
    return lax.broadcasted_iota(jnp.int32, shape, dim)


def piece_of(frame):
    return (frame * 2185) >> 16


def mm(a, b):
    return jnp.dot(a, b, preferred_element_type=jnp.float32)


def log_ratio(values):
    clipped = jnp.clip(values, -CLIP_LEVEL, CLIP_LEVEL)
    return jnp.log(1.0 + clipped) - jnp.log(1.0 - clipped)


def split(values):
    high = values.astype(jnp.bfloat16).astype(jnp.float32)
    return high, values - high


def kernel(
    n_blk, n_wide, series_hbm, mask_hbm, seed_hbm, out,
    series, mask, seed_index, seed_block, panel, others, own_stat, other_stats, pairs, spans, seeds,
    seed_stats, across, mask_across, rhs, whole_rhs, lhs, acc1, acc2,
    load_sem, seed_send, seed_recv, row_send, row_recv, stat_send, stat_recv,
):
    rows, frames = series.shape
    own = seed_index.shape[0]
    size = n_wide * own
    low = panel.shape[2]
    high = frames - low
    me_b = lax.axis_index("blk")
    me_w = lax.axis_index("wide")

    loads = [
        pltpu.make_async_copy(seed_hbm, seed_index, load_sem.at[0]),
        pltpu.make_async_copy(mask_hbm, mask, load_sem.at[1]),
        pltpu.make_async_copy(series_hbm, series, load_sem.at[2]),
    ]
    for copy in loads:
        copy.start()
    barrier = pltpu.get_barrier_semaphore()
    for d in range(1, n_wide):
        pl.semaphore_signal(
            barrier, inc=1, device_id=(me_b, lax.rem(me_w + d, n_wide)), device_id_type=MESH
        )
    for d in range(1, n_blk):
        pl.semaphore_signal(
            barrier, inc=1, device_id=(lax.rem(me_b + d, n_blk), me_w), device_id_type=MESH
        )

    frame_piece = piece_of(iota((frames, 2 * LANES), 0))
    lane = iota((frames, 2 * LANES), 1)
    wanted_piece = (lane & 31) + (lane >> 7)
    pairs[...] = jnp.where(frame_piece == wanted_piece, 1.0, 0.0).astype(jnp.bfloat16)
    row_piece = piece_of(iota((frames, frames), 0))
    column_piece = piece_of(iota((frames, frames), 1))
    spans[...] = jnp.where(row_piece == column_piece, 1.0, 0.0).astype(jnp.bfloat16)
    for copy in loads:
        copy.wait()
    weight = mask[...].reshape(1, frames).astype(jnp.float32)
    weight_rows = jnp.broadcast_to(weight, (16, frames)).astype(jnp.bfloat16)
    counts = mm(weight_rows, pairs[...])
    count1, count2 = counts[:1, :LANES], counts[:1, LANES:]
    count = jnp.maximum(count1 + count2, 1.0)
    between = count1 * count2 / count
    count1, count2 = jnp.maximum(count1, 1.0), jnp.maximum(count2, 1.0)
    inverse_count = 1.0 / jnp.maximum(mm(weight_rows, spans[...])[:1], 1.0)
    total_valid = jnp.sum(weight, axis=1, keepdims=True)

    def stats(values):
        kept = values * weight
        kept16 = kept.astype(jnp.bfloat16)
        sums = mm(kept16, pairs[...])
        sum1, sum2 = sums[:, :LANES], sums[:, LANES:]
        inner = (values - mm(kept16, spans[...]) * inverse_count) * weight
        inner = (inner * inner).astype(jnp.bfloat16)
        inner = mm(inner, pairs[:, :LANES] + pairs[:, LANES:])
        step = sum1 / count1 - sum2 / count2
        spread = inner + between * step * step
        mean = (sum1 + sum2) / count
        mean_all = jnp.sum(kept, axis=1, keepdims=True) / total_valid
        centred = (values - mean_all) * weight
        spread_all = jnp.sum(centred * centred, axis=1, keepdims=True)
        at = iota(mean.shape, 1)
        whole = (at & 31) == SPAN
        mean_high, mean_low = split(jnp.where(whole, mean_all, mean))
        inverse = lax.rsqrt(jnp.where(whole, spread_all, spread) + EPSILON)
        inverse_high, inverse_low = split(inverse)
        means = jnp.where(at < 32, mean_high, mean_low)
        return jnp.where(at < 64, means, jnp.where(at < 96, inverse_high, inverse_low))

    base = (me_b * n_wide + me_w) * rows
    row = iota((2 * own, rows), 0) & (own - 1)
    wanted = jnp.zeros((2 * own, rows), jnp.int32)
    for i in range(own):
        wanted = jnp.where(row == i, seed_index[i] - base, wanted)
    pick = jnp.where(iota((2 * own, rows), 1) == wanted, 1.0, 0.0).astype(jnp.bfloat16)
    picked = mm(pick, series[...])
    tail = jnp.concatenate([picked[:, low:], stats(picked)], axis=1)
    block = jnp.where(iota((2 * own, low), 0) < own, picked[:, :low], tail)
    seed_block[...] = block.astype(jnp.bfloat16)

    pl.semaphore_wait(barrier, n_wide + n_blk - 2)
    seed_copies = []
    for d in range(1, n_wide):
        copy = pltpu.make_async_remote_copy(
            src_ref=seed_block, dst_ref=panel.at[d - 1],
            send_sem=seed_send.at[d - 1], recv_sem=seed_recv.at[d - 1],
            device_id=(me_b, lax.rem(me_w + d, n_wide)), device_id_type=MESH,
        )
        copy.start()
        seed_copies.append(copy)

    def to_group(source, buffer, send, recv):
        copies = []
        for d in range(1, n_blk):
            copy = pltpu.make_async_remote_copy(
                src_ref=source, dst_ref=buffer.at[d - 1],
                send_sem=send.at[d - 1], recv_sem=recv.at[d - 1],
                device_id=(lax.rem(me_b + d, n_blk), me_w), device_id_type=MESH,
            )
            copy.start()
            copies.append(copy)
        return copies

    row_copies = to_group(series, others, row_send, row_recv)

    def load_target(block16, stat):
        lhs[0, :, :frames] = block16
        shift = pltpu.roll(block16.astype(jnp.float32), frames - HALF, 1)
        lhs[1, :, :frames] = shift.astype(jnp.bfloat16)
        lhs[0, :, frames:] = stat

    own_stat[...] = stats(series[...].astype(jnp.float32)).astype(jnp.bfloat16)
    stat_copies = to_group(own_stat, other_stats, stat_send, stat_recv)
    load_target(series[...], own_stat[...])

    select = iota((LANES, size), 0)

    def choose(n):
        return jnp.where((select == 64 + n) | (select == 96 + n), 1.0, 0.0).astype(jnp.bfloat16)

    zeros = jnp.zeros((LANES, size), jnp.bfloat16)
    for n in range(NWIN):
        rhs[n, :LANES, :size] = zeros
        rhs[n, :LANES, size:] = zeros
        rhs[n, LANES:, :size] = zeros
        rhs[n, LANES:, size:] = choose(n)
    whole_rhs[:frames, size:] = jnp.zeros((frames, size), jnp.bfloat16)
    whole_rhs[frames:, size:] = choose(SPAN)
    mask_across[...] = jnp.broadcast_to(weight, (LANES, frames)).T

    def unpack(block16, source):
        values = block16.astype(jnp.float32)
        at = pl.ds(pl.multiple_of(source * own, own), own)
        seeds[at, :low] = values[:own]
        seeds[at, low:] = values[own:, :high]
        seed_stats[at, :] = values[own:, high:]

    unpack(seed_block[...], me_w)
    for d in range(1, n_wide):
        seed_copies[d - 1].wait_recv()
        unpack(panel[d - 1], lax.rem(me_w + n_wide - d, n_wide))

    across[...] = seeds[...].T
    stat_across = seed_stats[...].T
    mean_across = stat_across[:32] + stat_across[32:64]
    inverse_across = stat_across[64:96] + stat_across[96:]

    def wide_mask(a, b):
        return jnp.concatenate([mask_across[a:b, :]] * (size // LANES), axis=1)

    for n in range(NWIN):
        first = n * STRIDE
        k = first // HALF * HALF
        a, b = first // 16 * 16, -(-(first + WIN) // 16) * 16
        frame = iota((b - a, size), 0) + a
        kept = jnp.where((frame >= first) & (frame < first + WIN), wide_mask(a, b), 0.0)
        window = (across[a:b, :] - mean_across[n : n + 1]) * kept * inverse_across[n : n + 1]
        window = window.astype(jnp.bfloat16)
        left = jnp.sum(window.astype(jnp.float32), axis=0, keepdims=True)
        rhs[n, a - k : b - k, :size] = window
        at = n // 16 * 16
        left = jnp.where(iota((16, size), 0) + at == n, -left, 0.0)
        rhs[n, LANES + at : LANES + at + 16, :size] = left.astype(jnp.bfloat16)
    whole = (across[...] - mean_across[SPAN : SPAN + 1]) * wide_mask(0, frames)
    whole = (whole * inverse_across[SPAN : SPAN + 1]).astype(jnp.bfloat16)
    left = jnp.sum(whole.astype(jnp.float32), axis=0, keepdims=True)
    whole_rhs[:frames, :size] = whole
    left = jnp.where((select == SPAN) | (select == 32 + SPAN), -left, 0.0)
    whole_rhs[frames:, :size] = left.astype(jnp.bfloat16)

    scale = jnp.sqrt(total_valid - 3.0) * 0.5

    def compare(slot):
        both = mm(lhs[0], whole_rhs[...])
        out[1, slot] = (scale * log_ratio(both[:, :size] * both[:, size:])).astype(jnp.bfloat16)
        acc1[...] = jnp.zeros_like(acc1)
        acc2[...] = jnp.zeros_like(acc2)
        group = 4

        def step(i, carry):
            first = second = None
            for g in range(group):
                n = i * group + g
                k = n * STRIDE // HALF
                at = pl.ds(pl.multiple_of(k // 2 * LANES, LANES), LANES)
                left = jnp.concatenate([lhs[k % 2, :, at], lhs[0, :, frames:]], axis=1)
                both = mm(left, rhs[n])
                z = log_ratio(both[:, :size] * both[:, size:])
                first = z if g == 0 else first + z
                second = z * z if g == 0 else second + z * z
            acc1[...] += first
            acc2[...] += second
            return carry

        lax.fori_loop(0, NWIN // group, step, 0)
        moment = acc1[...] * (0.5 / NWIN)
        spread = acc2[...] * (0.25 / NWIN) - moment * moment
        out[0, slot] = ((WIN - 3) * spread).astype(jnp.bfloat16)

    compare(me_b)
    for d in range(1, n_blk):
        row_copies[d - 1].wait_recv()
        stat_copies[d - 1].wait_recv()
        load_target(others[d - 1], other_stats[d - 1])
        compare(lax.rem(me_b + n_blk - d, n_blk))

    for copy in seed_copies + row_copies + stat_copies:
        copy.wait_send()


def solution(mesh):
    n_blk, n_wide = mesh.shape["blk"], mesh.shape["wide"]

    def body(series, scrub_mask, seed_index):
        rows, frames = series.shape
        own = seed_index.shape[0]
        size = n_wide * own
        low = (frames // LANES + 1) // 2 * LANES
        hbm = pl.BlockSpec(memory_space=pltpu.HBM)
        out = pl.pallas_call(
            functools.partial(kernel, n_blk, n_wide),
            out_shape=jax.ShapeDtypeStruct((2, n_blk, rows, size), jnp.bfloat16),
            in_specs=[hbm, hbm, hbm],
            out_specs=pl.BlockSpec(memory_space=pltpu.VMEM),
            scratch_shapes=[
                pltpu.VMEM((rows, frames), jnp.bfloat16),
                pltpu.VMEM((frames,), jnp.int32),
                pltpu.SMEM((own,), jnp.int32),
                pltpu.VMEM((2 * own, low), jnp.bfloat16),
                pltpu.VMEM((n_wide - 1, 2 * own, low), jnp.bfloat16),
                pltpu.VMEM((n_blk - 1, rows, frames), jnp.bfloat16),
                pltpu.VMEM((rows, LANES), jnp.bfloat16),
                pltpu.VMEM((n_blk - 1, rows, LANES), jnp.bfloat16),
                pltpu.VMEM((frames, 2 * LANES), jnp.bfloat16),
                pltpu.VMEM((frames, frames), jnp.bfloat16),
                pltpu.VMEM((size, frames), jnp.float32),
                pltpu.VMEM((size, LANES), jnp.float32),
                pltpu.VMEM((frames, size), jnp.float32),
                pltpu.VMEM((frames, LANES), jnp.float32),
                pltpu.VMEM((NWIN, 2 * LANES, 2 * size), jnp.bfloat16),
                pltpu.VMEM((frames + LANES, 2 * size), jnp.bfloat16),
                pltpu.VMEM((2, rows, frames + LANES), jnp.bfloat16),
                pltpu.VMEM((rows, size), jnp.float32),
                pltpu.VMEM((rows, size), jnp.float32),
                pltpu.SemaphoreType.DMA((3,)),
                pltpu.SemaphoreType.DMA((n_wide - 1,)),
                pltpu.SemaphoreType.DMA((n_wide - 1,)),
                pltpu.SemaphoreType.DMA((n_blk - 1,)),
                pltpu.SemaphoreType.DMA((n_blk - 1,)),
                pltpu.SemaphoreType.DMA((n_blk - 1,)),
                pltpu.SemaphoreType.DMA((n_blk - 1,)),
            ],
            compiler_params=pltpu.CompilerParams(
                collective_id=0, has_side_effects=True, vmem_limit_bytes=63 * 2**20
            ),
            cost_estimate=pl.CostEstimate(
                flops=n_blk * rows * size * 2 * 1800, bytes_accessed=2**20, transcendentals=0
            ),
        )(series, scrub_mask, seed_index)
        return out[0], out[1]

    in_specs = (P(("blk", "wide"), None), P(), P(("blk", "wide")))
    out_specs = (P(None, "wide", "blk"), P(None, "wide", "blk"))
    return jax.shard_map(body, mesh=mesh, in_specs=in_specs, out_specs=out_specs, check_vma=False)
```

```python
import functools

import jax
import jax.numpy as jnp
from jax import lax
from jax.experimental import pallas as pl
from jax.experimental.pallas import tpu as pltpu
from jax.sharding import PartitionSpec as P

WIN = 60
STRIDE = 30
NWIN = 20
SPAN = 21
EPSILON = 1e-05
CLIP_LEVEL = 0.99
LANES = 128
HALF = 64
MESH = pl.DeviceIdType.MESH
NT = (((1,), (1,)), ((), ()))


def iota(shape, dim):
    return lax.broadcasted_iota(jnp.int32, shape, dim)


def piece_of(frame):
    return (frame * 2185) >> 16


def mm(a, b):
    return jnp.dot(a, b, preferred_element_type=jnp.float32)


def log_ratio(values):
    clipped = jnp.clip(values, -CLIP_LEVEL, CLIP_LEVEL)
    return jnp.log(1.0 + clipped) - jnp.log(1.0 - clipped)


def split(values):
    high = values.astype(jnp.bfloat16).astype(jnp.float32)
    return high, values - high


def kernel(
    n_blk, n_wide, series_hbm, mask_hbm, seed_hbm, out,
    series, mask, seed_index, seed_block, panel, others, own_stat, other_stats, pairs, spans, seeds,
    seed_stats, across, mask_across, rhs, whole_rhs, lhs, acc1, acc2,
    load_sem, seed_send, seed_recv, row_send, row_recv, stat_send, stat_recv,
):
    rows, frames = series.shape
    own = seed_index.shape[0]
    size = n_wide * own
    low = panel.shape[2]
    high = frames - low
    me_b = lax.axis_index("blk")
    me_w = lax.axis_index("wide")

    loads = [
        pltpu.make_async_copy(seed_hbm, seed_index, load_sem.at[0]),
        pltpu.make_async_copy(mask_hbm, mask, load_sem.at[1]),
        pltpu.make_async_copy(series_hbm, series, load_sem.at[2]),
    ]
    for copy in loads:
        copy.start()
    barrier = pltpu.get_barrier_semaphore()
    half = n_wide // 2
    sibling = me_w + 1 - 2 * lax.rem(me_w, 2)
    peers = [lax.rem(me_w + 2 * d, n_wide) for d in range(1, half)]
    for peer in [sibling] + peers:
        pl.semaphore_signal(barrier, inc=1, device_id=(me_b, peer), device_id_type=MESH)
    for d in range(1, n_blk):
        pl.semaphore_signal(
            barrier, inc=1, device_id=(lax.rem(me_b + d, n_blk), me_w), device_id_type=MESH
        )

    frame_piece = piece_of(iota((frames, 2 * LANES), 0))
    lane = iota((frames, 2 * LANES), 1)
    wanted_piece = (lane & 31) + (lane >> 7)
    pairs[...] = jnp.where(frame_piece == wanted_piece, 1.0, 0.0).astype(jnp.bfloat16)
    row_piece = piece_of(iota((frames, frames), 0))
    column_piece = piece_of(iota((frames, frames), 1))
    spans[...] = jnp.where(row_piece == column_piece, 1.0, 0.0).astype(jnp.bfloat16)
    for copy in loads:
        copy.wait()
    weight = mask[...].reshape(1, frames).astype(jnp.float32)
    weight_rows = jnp.broadcast_to(weight, (16, frames)).astype(jnp.bfloat16)
    counts = mm(weight_rows, pairs[...])
    count1, count2 = counts[:1, :LANES], counts[:1, LANES:]
    count = jnp.maximum(count1 + count2, 1.0)
    between = count1 * count2 / count
    count1, count2 = jnp.maximum(count1, 1.0), jnp.maximum(count2, 1.0)
    inverse_count = 1.0 / jnp.maximum(mm(weight_rows, spans[...])[:1], 1.0)
    total_valid = jnp.sum(weight, axis=1, keepdims=True)

    def stats(values):
        kept = values * weight
        kept16 = kept.astype(jnp.bfloat16)
        sums = mm(kept16, pairs[...])
        sum1, sum2 = sums[:, :LANES], sums[:, LANES:]
        inner = (values - mm(kept16, spans[...]) * inverse_count) * weight
        inner = (inner * inner).astype(jnp.bfloat16)
        inner = mm(inner, pairs[:, :LANES] + pairs[:, LANES:])
        step = sum1 / count1 - sum2 / count2
        spread = inner + between * step * step
        mean = (sum1 + sum2) / count
        mean_all = jnp.sum(kept, axis=1, keepdims=True) / total_valid
        centred = (values - mean_all) * weight
        spread_all = jnp.sum(centred * centred, axis=1, keepdims=True)
        at = iota(mean.shape, 1)
        whole = (at & 31) == SPAN
        mean_high, mean_low = split(jnp.where(whole, mean_all, mean))
        inverse = lax.rsqrt(jnp.where(whole, spread_all, spread) + EPSILON)
        inverse_high, inverse_low = split(inverse)
        means = jnp.where(at < 32, mean_high, mean_low)
        return jnp.where(at < 64, means, jnp.where(at < 96, inverse_high, inverse_low))

    base = (me_b * n_wide + me_w) * rows
    row = iota((2 * own, rows), 0) & (own - 1)
    wanted = jnp.zeros((2 * own, rows), jnp.int32)
    for i in range(own):
        wanted = jnp.where(row == i, seed_index[i] - base, wanted)
    pick = jnp.where(iota((2 * own, rows), 1) == wanted, 1.0, 0.0).astype(jnp.bfloat16)
    picked = mm(pick, series[...])
    tail = jnp.concatenate([picked[:, low:], stats(picked)], axis=1)
    block = jnp.where(iota((2 * own, low), 0) < own, picked[:, :low], tail)
    seed_block[...] = block.astype(jnp.bfloat16)

    pl.semaphore_wait(barrier, half + n_blk - 1)

    def send_seeds(source, slot, target):
        copy = pltpu.make_async_remote_copy(
            src_ref=source, dst_ref=panel.at[slot],
            send_sem=seed_send.at[slot], recv_sem=seed_recv.at[slot],
            device_id=(me_b, target), device_id_type=MESH,
        )
        copy.start()
        return copy

    direct = [send_seeds(seed_block, d, peers[d]) for d in range(half - 1)]
    passed = [send_seeds(seed_block, half - 1, sibling)]

    def to_group(source, buffer, send, recv):
        copies = []
        for d in range(1, n_blk):
            copy = pltpu.make_async_remote_copy(
                src_ref=source, dst_ref=buffer.at[d - 1],
                send_sem=send.at[d - 1], recv_sem=recv.at[d - 1],
                device_id=(lax.rem(me_b + d, n_blk), me_w), device_id_type=MESH,
            )
            copy.start()
            copies.append(copy)
        return copies

    row_copies = to_group(series, others, row_send, row_recv)

    def load_target(block16, stat):
        lhs[0, :, :frames] = block16
        shift = pltpu.roll(block16.astype(jnp.float32), frames - HALF, 1)
        lhs[1, :, :frames] = shift.astype(jnp.bfloat16)
        lhs[0, :, frames:] = stat

    own_stat[...] = stats(series[...].astype(jnp.float32)).astype(jnp.bfloat16)
    stat_copies = to_group(own_stat, other_stats, stat_send, stat_recv)
    load_target(series[...], own_stat[...])

    select = iota((LANES, size), 0)

    def choose(n):
        return jnp.where((select == 64 + n) | (select == 96 + n), 1.0, 0.0).astype(jnp.bfloat16)

    zeros = jnp.zeros((LANES, size), jnp.bfloat16)
    for n in range(NWIN):
        rhs[n, :LANES, :size] = zeros
        rhs[n, :LANES, size:] = zeros
        rhs[n, LANES:, :size] = zeros
        rhs[n, LANES:, size:] = choose(n)
    whole_rhs[:frames, size:] = jnp.zeros((frames, size), jnp.bfloat16)
    whole_rhs[frames:, size:] = choose(SPAN)
    mask_across[...] = jnp.broadcast_to(weight, (LANES, frames)).T

    def unpack(block16, source):
        values = block16.astype(jnp.float32)
        at = pl.ds(pl.multiple_of(source * own, own), own)
        seeds[at, :low] = values[:own]
        seeds[at, low:] = values[own:, :high]
        seed_stats[at, :] = values[own:, high:]

    for d in range(half - 1):
        direct[d].wait_recv()
        passed.append(send_seeds(panel.at[d], half + d, sibling))
    unpack(seed_block[...], me_w)
    for d in range(half - 1):
        unpack(panel[d], lax.rem(me_w + n_wide - 2 * (d + 1), n_wide))
    for d in range(half):
        passed[d].wait_recv()
        unpack(panel[half - 1 + d], lax.rem(sibling + n_wide - 2 * d, n_wide))

    across[...] = seeds[...].T
    stat_across = seed_stats[...].T
    mean_across = stat_across[:32] + stat_across[32:64]
    inverse_across = stat_across[64:96] + stat_across[96:]

    def wide_mask(a, b):
        return jnp.concatenate([mask_across[a:b, :]] * (size // LANES), axis=1)

    for n in range(NWIN):
        first = n * STRIDE
        k = first // HALF * HALF
        a, b = first // 16 * 16, -(-(first + WIN) // 16) * 16
        frame = iota((b - a, size), 0) + a
        kept = jnp.where((frame >= first) & (frame < first + WIN), wide_mask(a, b), 0.0)
        window = (across[a:b, :] - mean_across[n : n + 1]) * kept * inverse_across[n : n + 1]
        window = window.astype(jnp.bfloat16)
        left = jnp.sum(window.astype(jnp.float32), axis=0, keepdims=True)
        rhs[n, a - k : b - k, :size] = window
        at = n // 16 * 16
        left = jnp.where(iota((16, size), 0) + at == n, -left, 0.0)
        rhs[n, LANES + at : LANES + at + 16, :size] = left.astype(jnp.bfloat16)
    whole = (across[...] - mean_across[SPAN : SPAN + 1]) * wide_mask(0, frames)
    whole = (whole * inverse_across[SPAN : SPAN + 1]).astype(jnp.bfloat16)
    left = jnp.sum(whole.astype(jnp.float32), axis=0, keepdims=True)
    whole_rhs[:frames, :size] = whole
    left = jnp.where((select == SPAN) | (select == 32 + SPAN), -left, 0.0)
    whole_rhs[frames:, :size] = left.astype(jnp.bfloat16)

    scale = jnp.sqrt(total_valid - 3.0) * 0.5

    def compare(slot):
        both = mm(lhs[0], whole_rhs[...])
        out[1, slot] = (scale * log_ratio(both[:, :size] * both[:, size:])).astype(jnp.bfloat16)
        acc1[...] = jnp.zeros_like(acc1)
        acc2[...] = jnp.zeros_like(acc2)
        group = 4

        def step(i, carry):
            first = second = None
            for g in range(group):
                n = i * group + g
                k = n * STRIDE // HALF
                at = pl.ds(pl.multiple_of(k // 2 * LANES, LANES), LANES)
                left = jnp.concatenate([lhs[k % 2, :, at], lhs[0, :, frames:]], axis=1)
                both = mm(left, rhs[n])
                z = log_ratio(both[:, :size] * both[:, size:])
                first = z if g == 0 else first + z
                second = z * z if g == 0 else second + z * z
            acc1[...] += first
            acc2[...] += second
            return carry

        lax.fori_loop(0, NWIN // group, step, 0)
        moment = acc1[...] * (0.5 / NWIN)
        spread = acc2[...] * (0.25 / NWIN) - moment * moment
        out[0, slot] = ((WIN - 3) * spread).astype(jnp.bfloat16)

    compare(me_b)
    for d in range(1, n_blk):
        row_copies[d - 1].wait_recv()
        stat_copies[d - 1].wait_recv()
        load_target(others[d - 1], other_stats[d - 1])
        compare(lax.rem(me_b + n_blk - d, n_blk))

    for copy in direct + passed + row_copies + stat_copies:
        copy.wait_send()


def deliver(both, dispersion, statistic, sem):
    copies = [
        pltpu.make_async_copy(both.at[0], dispersion, sem.at[0]),
        pltpu.make_async_copy(both.at[1], statistic, sem.at[1]),
    ]
    for copy in copies:
        copy.start()
    for copy in copies:
        copy.wait()


def solution(mesh):
    n_blk, n_wide = mesh.shape["blk"], mesh.shape["wide"]

    def body(series, scrub_mask, seed_index):
        rows, frames = series.shape
        own = seed_index.shape[0]
        size = n_wide * own
        low = (frames // LANES + 1) // 2 * LANES
        hbm = pl.BlockSpec(memory_space=pltpu.HBM)
        out = pl.pallas_call(
            functools.partial(kernel, n_blk, n_wide),
            out_shape=jax.ShapeDtypeStruct((2, n_blk, rows, size), jnp.bfloat16),
            in_specs=[hbm, hbm, hbm],
            out_specs=pl.BlockSpec(memory_space=pltpu.VMEM),
            scratch_shapes=[
                pltpu.VMEM((rows, frames), jnp.bfloat16),
                pltpu.VMEM((frames,), jnp.int32),
                pltpu.SMEM((own,), jnp.int32),
                pltpu.VMEM((2 * own, low), jnp.bfloat16),
                pltpu.VMEM((n_wide - 1, 2 * own, low), jnp.bfloat16),
                pltpu.VMEM((n_blk - 1, rows, frames), jnp.bfloat16),
                pltpu.VMEM((rows, LANES), jnp.bfloat16),
                pltpu.VMEM((n_blk - 1, rows, LANES), jnp.bfloat16),
                pltpu.VMEM((frames, 2 * LANES), jnp.bfloat16),
                pltpu.VMEM((frames, frames), jnp.bfloat16),
                pltpu.VMEM((size, frames), jnp.float32),
                pltpu.VMEM((size, LANES), jnp.float32),
                pltpu.VMEM((frames, size), jnp.float32),
                pltpu.VMEM((frames, LANES), jnp.float32),
                pltpu.VMEM((NWIN, 2 * LANES, 2 * size), jnp.bfloat16),
                pltpu.VMEM((frames + LANES, 2 * size), jnp.bfloat16),
                pltpu.VMEM((2, rows, frames + LANES), jnp.bfloat16),
                pltpu.VMEM((rows, size), jnp.float32),
                pltpu.VMEM((rows, size), jnp.float32),
                pltpu.SemaphoreType.DMA((3,)),
                pltpu.SemaphoreType.DMA((n_wide - 1,)),
                pltpu.SemaphoreType.DMA((n_wide - 1,)),
                pltpu.SemaphoreType.DMA((n_blk - 1,)),
                pltpu.SemaphoreType.DMA((n_blk - 1,)),
                pltpu.SemaphoreType.DMA((n_blk - 1,)),
                pltpu.SemaphoreType.DMA((n_blk - 1,)),
            ],
            compiler_params=pltpu.CompilerParams(
                collective_id=0, has_side_effects=True, vmem_limit_bytes=63 * 2**20
            ),
            cost_estimate=pl.CostEstimate(
                flops=n_blk * rows * size * 2 * 1800, bytes_accessed=2**20, transcendentals=0
            ),
        )(series, scrub_mask, seed_index)
        half = jax.ShapeDtypeStruct((n_blk, rows, size), jnp.bfloat16)
        return pl.pallas_call(
            deliver,
            out_shape=(half, half),
            in_specs=[hbm],
            out_specs=(hbm, hbm),
            scratch_shapes=[pltpu.SemaphoreType.DMA((2,))],
            compiler_params=pltpu.CompilerParams(vmem_limit_bytes=63 * 2**20),
        )(out)

    in_specs = (P(("blk", "wide"), None), P(), P(("blk", "wide")))
    out_specs = (P(None, "wide", "blk"), P(None, "wide", "blk"))
    return jax.shard_map(body, mesh=mesh, in_specs=in_specs, out_specs=out_specs, check_vma=False)
```

```python
import functools

import jax
import jax.numpy as jnp
from jax import lax
from jax.experimental import pallas as pl
from jax.experimental.pallas import tpu as pltpu
from jax.sharding import PartitionSpec as P

WIN = 60
STRIDE = 30
NWIN = 20
SPAN = 21
EPSILON = 1e-05
CLIP_LEVEL = 0.99
LANES = 128
HALF = 64
MESH = pl.DeviceIdType.MESH
NT = (((1,), (1,)), ((), ()))


def iota(shape, dim):
    return lax.broadcasted_iota(jnp.int32, shape, dim)


def piece_of(frame):
    return (frame * 2185) >> 16


def mm(a, b):
    return jnp.dot(a, b, preferred_element_type=jnp.float32)


def log_ratio(values):
    clipped = jnp.clip(values, -CLIP_LEVEL, CLIP_LEVEL)
    return jnp.log(1.0 + clipped) - jnp.log(1.0 - clipped)


def split(values):
    high = values.astype(jnp.bfloat16).astype(jnp.float32)
    return high, values - high


def kernel(
    n_blk, n_wide, series_hbm, mask_hbm, seed_hbm, out,
    series, mask, seed_index, seed_block, panel, others, own_stat, other_stats, pairs, spans, seeds,
    seed_stats, across, mask_across, rhs, whole_rhs, lhs, acc1, acc2,
    load_sem, seed_send, seed_recv, row_send, row_recv, stat_send, stat_recv,
):
    rows, frames = series.shape
    own = seed_index.shape[0]
    size = n_wide * own
    low = panel.shape[2]
    high = frames - low
    me_b = lax.axis_index("blk")
    me_w = lax.axis_index("wide")

    loads = [
        pltpu.make_async_copy(seed_hbm, seed_index, load_sem.at[0]),
        pltpu.make_async_copy(mask_hbm, mask, load_sem.at[1]),
        pltpu.make_async_copy(series_hbm, series, load_sem.at[2]),
    ]
    for copy in loads:
        copy.start()
    barrier = pltpu.get_barrier_semaphore()
    half = n_wide // 2
    sibling = me_w + 1 - 2 * lax.rem(me_w, 2)
    peers = [lax.rem(me_w + 2 * d, n_wide) for d in range(1, half)]
    for peer in [sibling] + peers:
        pl.semaphore_signal(barrier, inc=1, device_id=(me_b, peer), device_id_type=MESH)
    for d in range(1, n_blk):
        pl.semaphore_signal(
            barrier, inc=1, device_id=(lax.rem(me_b + d, n_blk), me_w), device_id_type=MESH
        )

    frame_piece = piece_of(iota((frames, 2 * LANES), 0))
    lane = iota((frames, 2 * LANES), 1)
    wanted_piece = (lane & 31) + (lane >> 7)
    pairs[...] = jnp.where(frame_piece == wanted_piece, 1.0, 0.0).astype(jnp.bfloat16)
    row_piece = piece_of(iota((frames, frames), 0))
    column_piece = piece_of(iota((frames, frames), 1))
    spans[...] = jnp.where(row_piece == column_piece, 1.0, 0.0).astype(jnp.bfloat16)
    for copy in loads:
        copy.wait()
    weight = mask[...].reshape(1, frames).astype(jnp.float32)
    weight_rows = jnp.broadcast_to(weight, (16, frames)).astype(jnp.bfloat16)
    counts = mm(weight_rows, pairs[...])
    count1, count2 = counts[:1, :LANES], counts[:1, LANES:]
    count = jnp.maximum(count1 + count2, 1.0)
    between = count1 * count2 / count
    count1, count2 = jnp.maximum(count1, 1.0), jnp.maximum(count2, 1.0)
    inverse_count = 1.0 / jnp.maximum(mm(weight_rows, spans[...])[:1], 1.0)
    total_valid = jnp.sum(weight, axis=1, keepdims=True)

    def stats(values):
        kept = values * weight
        kept16 = kept.astype(jnp.bfloat16)
        sums = mm(kept16, pairs[...])
        sum1, sum2 = sums[:, :LANES], sums[:, LANES:]
        inner = (values - mm(kept16, spans[...]) * inverse_count) * weight
        inner = (inner * inner).astype(jnp.bfloat16)
        inner = mm(inner, pairs[:, :LANES] + pairs[:, LANES:])
        step = sum1 / count1 - sum2 / count2
        spread = inner + between * step * step
        mean = (sum1 + sum2) / count
        mean_all = jnp.sum(kept, axis=1, keepdims=True) / total_valid
        centred = (values - mean_all) * weight
        spread_all = jnp.sum(centred * centred, axis=1, keepdims=True)
        at = iota(mean.shape, 1)
        whole = (at & 31) == SPAN
        mean_high, mean_low = split(jnp.where(whole, mean_all, mean))
        inverse = lax.rsqrt(jnp.where(whole, spread_all, spread) + EPSILON)
        inverse_high, inverse_low = split(inverse)
        means = jnp.where(at < 32, mean_high, mean_low)
        return jnp.where(at < 64, means, jnp.where(at < 96, inverse_high, inverse_low))

    base = (me_b * n_wide + me_w) * rows
    row = iota((2 * own, rows), 0) & (own - 1)
    wanted = jnp.zeros((2 * own, rows), jnp.int32)
    for i in range(own):
        wanted = jnp.where(row == i, seed_index[i] - base, wanted)
    pick = jnp.where(iota((2 * own, rows), 1) == wanted, 1.0, 0.0).astype(jnp.bfloat16)
    picked = mm(pick, series[...])
    tail = jnp.concatenate([picked[:, low:], stats(picked)], axis=1)
    block = jnp.where(iota((2 * own, low), 0) < own, picked[:, :low], tail)
    seed_block[...] = block.astype(jnp.bfloat16)

    pl.semaphore_wait(barrier, half + n_blk - 1)

    def send_seeds(source, slot, target):
        copy = pltpu.make_async_remote_copy(
            src_ref=source, dst_ref=panel.at[slot],
            send_sem=seed_send.at[slot], recv_sem=seed_recv.at[slot],
            device_id=(me_b, target), device_id_type=MESH,
        )
        copy.start()
        return copy

    direct = [send_seeds(seed_block, d, peers[d]) for d in range(half - 1)]
    passed = [send_seeds(seed_block, half - 1, sibling)]

    def to_group(source, buffer, send, recv, d):
        return pltpu.make_async_remote_copy(
            src_ref=source, dst_ref=buffer.at[d - 1],
            send_sem=send.at[d - 1], recv_sem=recv.at[d - 1],
            device_id=(lax.rem(me_b + d, n_blk), me_w), device_id_type=MESH,
        )

    def row_copy(d):
        return to_group(series, others, row_send, row_recv, d)

    def stat_copy(d):
        return to_group(own_stat, other_stats, stat_send, stat_recv, d)

    for d in range(1, n_blk):
        row_copy(d).start()

    def load_target(block16, stat):
        lhs[0, :, :frames] = block16
        shift = pltpu.roll(block16.astype(jnp.float32), frames - HALF, 1)
        lhs[1, :, :frames] = shift.astype(jnp.bfloat16)
        lhs[0, :, frames:] = stat

    own_stat[...] = stats(series[...].astype(jnp.float32)).astype(jnp.bfloat16)
    for d in range(1, n_blk):
        stat_copy(d).start()
    load_target(series[...], own_stat[...])

    select = iota((LANES, size), 0)

    def choose(n):
        return jnp.where((select == 64 + n) | (select == 96 + n), 1.0, 0.0).astype(jnp.bfloat16)

    zeros = jnp.zeros((LANES, size), jnp.bfloat16)
    for n in range(NWIN):
        rhs[n, :LANES, :size] = zeros
        rhs[n, :LANES, size:] = zeros
        rhs[n, LANES:, :size] = zeros
        rhs[n, LANES:, size:] = choose(n)
    whole_rhs[:frames, size:] = jnp.zeros((frames, size), jnp.bfloat16)
    whole_rhs[frames:, size:] = choose(SPAN)
    mask_across[...] = jnp.broadcast_to(weight, (LANES, frames)).T

    def unpack(block16, source):
        values = block16.astype(jnp.float32)
        at = pl.ds(pl.multiple_of(source * own, own), own)
        seeds[at, :low] = values[:own]
        seeds[at, low:] = values[own:, :high]
        seed_stats[at, :] = values[own:, high:]

    for d in range(half - 1):
        direct[d].wait_recv()
        passed.append(send_seeds(panel.at[d], half + d, sibling))
    unpack(seed_block[...], me_w)
    for d in range(half - 1):
        unpack(panel[d], lax.rem(me_w + n_wide - 2 * (d + 1), n_wide))
    for d in range(half):
        passed[d].wait_recv()
        unpack(panel[half - 1 + d], lax.rem(sibling + n_wide - 2 * d, n_wide))

    across[...] = seeds[...].T
    stat_across = seed_stats[...].T
    mean_across = stat_across[:32] + stat_across[32:64]
    inverse_across = stat_across[64:96] + stat_across[96:]

    def wide_mask(a, b):
        return jnp.concatenate([mask_across[a:b, :]] * (size // LANES), axis=1)

    for n in range(NWIN):
        first = n * STRIDE
        k = first // HALF * HALF
        a, b = first // 16 * 16, -(-(first + WIN) // 16) * 16
        frame = iota((b - a, size), 0) + a
        kept = jnp.where((frame >= first) & (frame < first + WIN), wide_mask(a, b), 0.0)
        window = (across[a:b, :] - mean_across[n : n + 1]) * kept * inverse_across[n : n + 1]
        window = window.astype(jnp.bfloat16)
        left = jnp.sum(window.astype(jnp.float32), axis=0, keepdims=True)
        rhs[n, a - k : b - k, :size] = window
        at = n // 16 * 16
        left = jnp.where(iota((16, size), 0) + at == n, -left, 0.0)
        rhs[n, LANES + at : LANES + at + 16, :size] = left.astype(jnp.bfloat16)
    whole = (across[...] - mean_across[SPAN : SPAN + 1]) * wide_mask(0, frames)
    whole = (whole * inverse_across[SPAN : SPAN + 1]).astype(jnp.bfloat16)
    left = jnp.sum(whole.astype(jnp.float32), axis=0, keepdims=True)
    whole_rhs[:frames, :size] = whole
    left = jnp.where((select == SPAN) | (select == 32 + SPAN), -left, 0.0)
    whole_rhs[frames:, :size] = left.astype(jnp.bfloat16)

    scale = jnp.sqrt(total_valid - 3.0) * 0.5

    def compare(slot):
        both = mm(lhs[0], whole_rhs[...])
        out[1, slot] = (scale * log_ratio(both[:, :size] * both[:, size:])).astype(jnp.bfloat16)
        group = 4
        for start in range(0, NWIN, group):
            first = second = None
            for n in range(start, start + group):
                k = n * STRIDE // HALF
                at = slice(k // 2 * LANES, k // 2 * LANES + LANES)
                left = jnp.concatenate([lhs[k % 2, :, at], lhs[0, :, frames:]], axis=1)
                both = mm(left, rhs[n])
                z = log_ratio(both[:, :size] * both[:, size:])
                first = z if n == start else first + z
                second = z * z if n == start else second + z * z
            acc1[...] = first if start == 0 else acc1[...] + first
            acc2[...] = second if start == 0 else acc2[...] + second
        moment = acc1[...] * (0.5 / NWIN)
        spread = acc2[...] * (0.25 / NWIN) - moment * moment
        out[0, slot] = ((WIN - 3) * spread).astype(jnp.bfloat16)

    compare(me_b)

    def other(d, carry):
        row_copy(d).wait_recv()
        stat_copy(d).wait_recv()
        load_target(others[d - 1], other_stats[d - 1])
        compare(lax.rem(me_b + n_blk - d, n_blk))
        return carry

    if n_blk == 2:
        other(1, 0)
    else:
        lax.fori_loop(1, n_blk, other, 0)

    for copy in direct + passed:
        copy.wait_send()
    for d in range(1, n_blk):
        row_copy(d).wait_send()
        stat_copy(d).wait_send()


def solution(mesh):
    n_blk, n_wide = mesh.shape["blk"], mesh.shape["wide"]

    def body(series, scrub_mask, seed_index):
        rows, frames = series.shape
        own = seed_index.shape[0]
        size = n_wide * own
        low = (frames // LANES + 1) // 2 * LANES
        hbm = pl.BlockSpec(memory_space=pltpu.HBM)
        out = pl.pallas_call(
            functools.partial(kernel, n_blk, n_wide),
            out_shape=jax.ShapeDtypeStruct((2, n_blk, rows, size), jnp.bfloat16),
            in_specs=[hbm, hbm, hbm],
            out_specs=pl.BlockSpec(memory_space=pltpu.VMEM),
            scratch_shapes=[
                pltpu.VMEM((rows, frames), jnp.bfloat16),
                pltpu.VMEM((frames,), jnp.int32),
                pltpu.SMEM((own,), jnp.int32),
                pltpu.VMEM((2 * own, low), jnp.bfloat16),
                pltpu.VMEM((n_wide - 1, 2 * own, low), jnp.bfloat16),
                pltpu.VMEM((n_blk - 1, rows, frames), jnp.bfloat16),
                pltpu.VMEM((rows, LANES), jnp.bfloat16),
                pltpu.VMEM((n_blk - 1, rows, LANES), jnp.bfloat16),
                pltpu.VMEM((frames, 2 * LANES), jnp.bfloat16),
                pltpu.VMEM((frames, frames), jnp.bfloat16),
                pltpu.VMEM((size, frames), jnp.float32),
                pltpu.VMEM((size, LANES), jnp.float32),
                pltpu.VMEM((frames, size), jnp.float32),
                pltpu.VMEM((frames, LANES), jnp.float32),
                pltpu.VMEM((NWIN, 2 * LANES, 2 * size), jnp.bfloat16),
                pltpu.VMEM((frames + LANES, 2 * size), jnp.bfloat16),
                pltpu.VMEM((2, rows, frames + LANES), jnp.bfloat16),
                pltpu.VMEM((rows, size), jnp.float32),
                pltpu.VMEM((rows, size), jnp.float32),
                pltpu.SemaphoreType.DMA((3,)),
                pltpu.SemaphoreType.DMA((n_wide - 1,)),
                pltpu.SemaphoreType.DMA((n_wide - 1,)),
                pltpu.SemaphoreType.DMA((n_blk - 1,)),
                pltpu.SemaphoreType.DMA((n_blk - 1,)),
                pltpu.SemaphoreType.DMA((n_blk - 1,)),
                pltpu.SemaphoreType.DMA((n_blk - 1,)),
            ],
            compiler_params=pltpu.CompilerParams(
                collective_id=0, has_side_effects=True, vmem_limit_bytes=63 * 2**20
            ),
            cost_estimate=pl.CostEstimate(
                flops=n_blk * rows * size * 2 * 1800, bytes_accessed=2**20, transcendentals=0
            ),
        )(series, scrub_mask, seed_index)
        return out[0], out[1]

    in_specs = (P(("blk", "wide"), None), P(), P(("blk", "wide")))
    out_specs = (P(None, "wide", "blk"), P(None, "wide", "blk"))
    return jax.shard_map(body, mesh=mesh, in_specs=in_specs, out_specs=out_specs, check_vma=False)
```
